32 devices in a mesh: rep: 1, ep: 32 (over z, y, x, core).
Axes of the slice: x: 2, y: 2, z: 4, core: 2. Of those that a mesh axis runs over, the one named last changes fastest.
Arguments:
- kv_cache: bfloat16 [128, 256, 576], P(('rep', 'ep')), may hold values from -6 to 6
- cache_len: int32 [128], P('rep'), may hold values from 1 to 254, 16384 in all
- move_slot: int32 [32, 2], P('rep'), may hold values from 0 to 3, as said below
- move_key: int32 [2], P('rep'), may hold values from 1 to 31
- queries: bfloat16 [2, 128, 128, 576], P(None, ('rep', 'ep')), may hold values from -150 to 150
- new_latent: bfloat16 [2, 128, 576], P(None, ('rep', 'ep')), may hold values from -6 to 6
- moe_in: bfloat16 [2, 128, 7168], P(None, ('rep', 'ep')), may hold values from -6 to 6
- expert_ids: int32 [2, 128, 1], P(None, ('rep', 'ep')), may hold values from 0 to 1; in each aligned block of 4 rows (0 to 3, 4 to 7, ..., all dimensions but the last counted through in order) at most 3 rows name the same one
- expert_weights: float32 [2, 128, 1], P(None, ('rep', 'ep')), may hold values from 0.25 to 1
- w_gate: bfloat16 [7168, 4096], P(None, 'ep'), may hold values from -0.0625 to 0.0625
- w_up: bfloat16 [7168, 4096], P(None, 'ep'), may hold values from -0.0625 to 0.0625
- w_down: bfloat16 [4096, 7168], P('ep'), may hold values from -0.125 to 0.125
Outputs:
- attention_out: bfloat16 [2, 128, 128, 512], P(None, ('rep', 'ep'))
- cache_out: bfloat16 [128, 256, 576], P(('rep', 'ep'))
- moe_out: bfloat16 [2, 128, 7168], P(None, ('rep', 'ep'))
The draws below stay inside these ranges and needn't reach their ends.
Inputs may be any that keep to these rules, and one draw needn't show every extreme that they name: `expert_ids`: in each step, no device routes more than 3 of its tokens to one expert; each token names different experts. `cache_len`: each request slot has at least one cached position; positions at and beyond its length are not part of it. `move_slot`: each row names 2 different slots. Move k pairs device i with device i XOR move_key[k].
All inputs are finite; a program needn't handle non-finite values.
Results may differ from the reference program's by a relative error of at most 0.0085.
Values may be sent and summed in bfloat16 or wider, within the bound.
A program may use at most 128 MiB of HBM per device.

```python
import math
import jax
import jax.numpy as jnp
import numpy as np
from jax import lax

D = 7168
FF = 2048
H = 128
LAT = 512
SPLIT = 16
STEPS = 2
TOK_DEV = 4
R_DEV = 4
L_MAX = 256
KVW = 576
FF_DEV = 128
EXPERTS = 2
TOPK = 1
CAP = 3
MIG = 2
N_REQ = 128
TOKENS = 128


def shared_latents(key):
    return jnp.clip(jax.random.normal(key, (STEPS, N_REQ, KVW), jnp.float32), -6.0, 6.0)


def draw_new_latent(key, part):
    latents = shared_latents(key)
    return latents.astype(jnp.bfloat16)


def draw_queries(key, part):
    key = jax.random.fold_in(key, 7)
    noise_key = jax.random.fold_in(key, 0)
    shape = (STEPS, N_REQ, H, KVW)
    noise = jnp.clip(jax.random.normal(noise_key, shape, jnp.float32), -6.0, 6.0)
    return noise.astype(jnp.bfloat16)


def draw_move_slot(key, part):
    key = jax.random.fold_in(key, 5)
    row_keys = jax.random.split(key, N_REQ // R_DEV)

    def one_order(row_key):
        return jax.random.permutation(row_key, R_DEV)
    orders = jax.vmap(one_order)(row_keys)
    return orders[:, :MIG].astype(jnp.int32)


def block_levels(own_key, shape, pieces, low, top_value):
    factor_of = 1.0
    for dim, blocks in pieces:
        draws = jax.random.uniform(jax.random.fold_in(jax.random.fold_in(own_key, 6), dim), (blocks,), jnp.float32, low / len(pieces), top_value / len(pieces))
        factor_of = factor_of * jnp.repeat(jnp.exp(draws), shape[dim] // blocks).reshape((-1,) + (1,) * (len(shape) - 1 - dim))
    return factor_of


def length_profile(amount, total, limit, slope):
    weights = [(1 << 20) // math.isqrt(standing ** slope) + 1 for standing in range(2, amount + 1)]
    spare, counts = total - limit - (amount - 1), [1] * (amount - 1)
    while spare > 0:
        free = [i for i in range(amount - 1) if counts[i] < limit]
        mass, left = sum([weights[i] for i in free]), spare
        for i in free:
            more = min(limit - counts[i], max(1, left * weights[i] // mass), spare)
            counts[i] = counts[i] + more
            spare = spare - more
    return np.array([limit] + counts)


def ragged_sizes(rng, count, total, reach, skew):
    if count == 2:
        one = jax.random.randint(rng, (), max(1, total - reach), min(reach, total - 1) + 1)
        return jnp.stack([one, total - one])
    tallies = jnp.asarray(length_profile(count, total, reach, skew), jnp.int32)
    pairs = (count - 1) // 2
    donor, receiver = tallies[1:1 + 2 * pairs:2], tallies[2:2 + 2 * pairs:2]
    margin = jnp.minimum(donor - 1, reach - receiver)
    shifted = jax.random.randint(jax.random.fold_in(rng, 1), (pairs,), 0, 1 << 20) % (margin + 1)
    tallies = tallies.at[1:1 + 2 * pairs:2].set(donor - shifted).at[2:2 + 2 * pairs:2].set(receiver + shifted)
    return tallies[jax.random.permutation(jax.random.fold_in(rng, 2), count)]


def assign_block(own_key, own, number, rows, count, top, most, slope):
    sequence = jax.random.permutation(own_key, count)
    crowded, ordinary = shares(count, rows * top, most, slope, True), shares(count, rows * top, most, slope, False)
    places = jnp.arange(count)

    def named(sizes, offset_by):
        used = int((sizes > 0).sum())
        fixed = max(1, used // 4)
        moved = fixed + (places - fixed + offset_by * (used - fixed)) % max(1, count - fixed)
        return jnp.zeros((count,), jnp.int32).at[sequence[jnp.where(places < fixed, places, moved)]].set(jnp.asarray(sizes, jnp.int32))

    sizes = jnp.where(number % 4 == 0, named(crowded, number // 4), named(ordinary, number - number // 4 - 1))
    mixed = jax.random.permutation(jax.random.fold_in(own, 3), count)
    giver, taker = mixed[0:count // 2 * 2:2], mixed[1:count // 2 * 2:2]
    margin = jnp.minimum(sizes[giver] - 1, most - sizes[taker]) // 2
    margin = jnp.where((giver == sequence[0]) | (taker == sequence[0]) | (sizes[taker] == 0), 0, jnp.maximum(margin, 0))
    moved = jax.random.randint(jax.random.fold_in(own, 4), (count // 2,), 0, 1 << 20) % (margin + 1)
    sizes = sizes.at[giver].add(-moved).at[taker].add(moved)
    labels = jnp.searchsorted(jnp.cumsum(sizes), jnp.arange(rows * top), side="right").astype(jnp.int32)
    listing = labels.reshape(top, rows).T
    listing = listing[jax.random.permutation(jax.random.fold_in(own, 1), rows)]
    offset_by = jax.random.randint(jax.random.fold_in(own, 2), (rows, 1), 0, top)
    return jnp.take_along_axis(listing, (jnp.arange(top)[None, :] + offset_by) % top, axis=1)


def shares(count, total, limit, slope, full):
    loads = [(1 << 20) // math.isqrt(grade ** slope) + 1 for grade in range(1, count + 1)]
    largest = limit if full else min(limit, max(-(-total // count), total * loads[0] // sum(loads)))
    least = 1 if total - largest >= count - 1 else 0
    holding, rest = [largest] + [least] * (count - 1), total - largest - least * (count - 1)
    while rest > 0:
        free = [i for i in range(1, count) if holding[i] < largest] or [i for i in range(1, count) if holding[i] < limit]
        mass, left = sum([loads[i] for i in free]), rest
        for i in free:
            extra = min(limit - holding[i], max(1, left * loads[i] // mass), rest)
            holding[i] = holding[i] + extra
            rest = rest - extra
    return np.array(holding)


def normal_values(own_key, shape, spread, reach, cuts=(), held_as=jnp.bfloat16):
    gain = block_levels(own_key, shape, cuts, -0.22, 0.18) if cuts else 1.0
    entries = jax.random.normal(own_key, shape, jnp.float32) * spread * gain
    return jnp.minimum(jnp.maximum(entries, -reach), reach).astype(held_as)


def setup_inputs(seed: int = 0, part: int = 0) -> dict:
    streams_of = jax.random.split(jax.random.key(seed), 13)
    own_keys = jax.random.split(jax.random.fold_in(streams_of[12], part), 13)
    kv_cache = normal_values(own_keys[0], (N_REQ, L_MAX, KVW), 1.0, 6.0, ((0, 32),))
    cache_len = ragged_sizes(own_keys[1], N_REQ, N_REQ * (L_MAX // 2), L_MAX - STEPS, 2).astype(jnp.int32)
    move_slot = draw_move_slot(jax.random.fold_in(jax.random.fold_in(streams_of[12], part), 71), part)
    move_key = jax.random.randint(own_keys[3], (MIG,), 1, N_REQ // R_DEV).astype(jnp.int32)
    queries = draw_queries(jax.random.fold_in(jax.random.fold_in(streams_of[12], part), 71), part)
    new_latent = draw_new_latent(jax.random.fold_in(jax.random.fold_in(streams_of[12], part), 71), part)
    moe_in = normal_values(own_keys[6], (STEPS, TOKENS, D), 1.0, 6.0, ((1, 32),))
    expert_ids_keys = jax.random.split(jax.random.fold_in(own_keys[7], 1), STEPS * TOKENS // TOK_DEV)
    expert_ids_turns = jax.random.permutation(jax.random.fold_in(own_keys[7], 3), STEPS * TOKENS // TOK_DEV)
    expert_ids = jax.vmap(lambda own, number: assign_block(jax.random.fold_in(own_keys[7], 2), own, number, TOK_DEV, EXPERTS, TOPK, CAP, 2))(expert_ids_keys, expert_ids_turns).reshape((STEPS, TOKENS, TOPK))
    expert_weights = jnp.clip(0.25 + 0.75 * jax.random.uniform(own_keys[8], (STEPS, TOKENS, TOPK), jnp.float32) ** block_levels(own_keys[8], (STEPS, TOKENS, TOPK), ((1, 32),), -0.2, 0.2), 0.25, 1.0)
    w_gate = normal_values(streams_of[9], (D, EXPERTS * FF), D ** -0.5, 0.0625, ((1, 32),))
    w_up = normal_values(streams_of[10], (D, EXPERTS * FF), D ** -0.5, 0.0625, ((1, 32),))
    w_down = normal_values(streams_of[11], (EXPERTS * FF, D), FF ** -0.5, 0.125, ((0, 32),))
    return dict(kv_cache=kv_cache, cache_len=cache_len, move_slot=move_slot, move_key=move_key, queries=queries, new_latent=new_latent, moe_in=moe_in, expert_ids=expert_ids, expert_weights=expert_weights, w_gate=w_gate, w_up=w_up, w_down=w_down)


softmax_scale = 192.0 ** -0.5


def migrate(kv_cache, cache_len, move_slot, move_key):
    devices = N_REQ // R_DEV
    by_device = kv_cache.reshape(devices, R_DEV, L_MAX, KVW)
    old_lengths = cache_len.reshape(devices, R_DEV)
    device_ids = jnp.arange(devices, dtype=jnp.int32)
    settled = by_device
    new_lengths = old_lengths
    for move_no in range(MIG):
        partner = jnp.bitwise_xor(device_ids, move_key[move_no]).astype(jnp.int32)
        source_slot = move_slot[partner, move_no]
        settled = settled.at[device_ids, move_slot[:, move_no]].set(by_device[partner, source_slot])
        new_lengths = new_lengths.at[device_ids, move_slot[:, move_no]].set(old_lengths[partner, source_slot])
    return settled.reshape(N_REQ, L_MAX, KVW), new_lengths.reshape(N_REQ)


def append_latents(cache_rows, lengths, fresh_rows):
    positions = jnp.arange(L_MAX, dtype=jnp.int32)
    for step_no in range(STEPS):
        target = positions[None, :] == (lengths + step_no)[:, None]
        cache_rows = jnp.where(target[:, :, None], fresh_rows[step_no][:, None, :], cache_rows)
    return cache_rows


def attend(queries, cache_rows, lengths):
    step_count, slot_count, head_count, row_width = queries.shape
    merged = jnp.transpose(queries, (1, 0, 2, 3)).reshape(slot_count, step_count * head_count, row_width)
    scores = jnp.einsum("rqc,rlc->rql", merged.astype(jnp.float32), cache_rows.astype(jnp.float32)) * softmax_scale
    positions = jnp.arange(cache_rows.shape[1], dtype=jnp.int32)
    step_of = jnp.arange(step_count * head_count, dtype=jnp.int32) // head_count
    visible = positions[None, None, :] < (lengths[:, None, None] + step_of[None, :, None] + 1)
    scores = jnp.where(visible, scores, jnp.float32(-1e30))
    row_max = jnp.max(scores, axis=-1, keepdims=True)
    weights = jnp.exp(scores - row_max)
    probabilities = (weights / jnp.sum(weights, axis=-1, keepdims=True)).astype(jnp.bfloat16)
    attended = jnp.einsum("rql,rlc->rqc", probabilities.astype(jnp.float32), cache_rows[:, :, :LAT].astype(jnp.float32))
    attended = attended.astype(jnp.bfloat16).reshape(slot_count, step_count, head_count, LAT)
    return jnp.transpose(attended, (1, 0, 2, 3))


def experts_apply(moe_in, expert_ids, expert_weights, w_gate, w_up, w_down):
    tokens = moe_in.reshape(STEPS * TOKENS, D)
    route_ids = expert_ids.reshape(STEPS * TOKENS, TOPK)
    route_gains = expert_weights.reshape(STEPS * TOKENS, TOPK)

    def add_expert(expert, running):
        expert = jnp.asarray(expert).astype(jnp.int32)
        gate_cols = lax.dynamic_slice_in_dim(w_gate, expert * FF, FF, 1)
        up_cols = lax.dynamic_slice_in_dim(w_up, expert * FF, FF, 1)
        down_rows = lax.dynamic_slice_in_dim(w_down, expert * FF, FF, 0)
        gate_act = jnp.dot(tokens, gate_cols, preferred_element_type=jnp.float32)
        up_act = jnp.dot(tokens, up_cols, preferred_element_type=jnp.float32)
        hidden = (jax.nn.silu(gate_act) * up_act).astype(jnp.bfloat16)

        def add_slice(slice_no, summed):
            slice_no = jnp.asarray(slice_no).astype(jnp.int32)
            hidden_part = lax.dynamic_slice_in_dim(hidden, slice_no * FF_DEV, FF_DEV, 1)
            down_part = lax.dynamic_slice_in_dim(down_rows, slice_no * FF_DEV, FF_DEV, 0)
            rounded = jnp.dot(hidden_part, down_part, preferred_element_type=jnp.float32).astype(jnp.bfloat16)
            return summed + lax.optimization_barrier(rounded).astype(jnp.float32)

        expert_out = lax.fori_loop(0, SPLIT, add_slice, jnp.zeros((STEPS * TOKENS, D), jnp.float32))
        weighting = jnp.sum(jnp.where(route_ids == expert, route_gains, jnp.float32(0.0)), axis=1)
        return running + weighting[:, None] * expert_out

    result = lax.fori_loop(0, EXPERTS, add_expert, jnp.zeros((STEPS * TOKENS, D), jnp.float32))
    return result.astype(jnp.bfloat16).reshape(STEPS, TOKENS, D)


def reference(kv_cache, cache_len, move_slot, move_key, queries, new_latent, moe_in, expert_ids, expert_weights, w_gate, w_up, w_down):
    settled, settled_len = migrate(kv_cache, cache_len, move_slot, move_key)
    cache_out = append_latents(settled, settled_len, new_latent)
    attention_out = attend(queries, cache_out, settled_len)
    moe_out = experts_apply(moe_in, expert_ids, expert_weights, w_gate, w_up, w_down)
    return attention_out, cache_out, moe_out
```

```python
import functools

import jax
import jax.numpy as jnp
from jax import lax
from jax.experimental import pallas as pl
from jax.experimental.pallas import tpu as pltpu
from jax.sharding import PartitionSpec as P

LAT = 512
SPLIT = 16
MESH = pl.DeviceIdType.MESH
LANES = 128
ORDERS = ((3, 1, 2), (1, 2, 3), (2, 3, 1))

softmax_scale = 192.0 ** (-0.5)


def flipped(index, distance):
    return index + distance * (1 - 2 * ((index // distance) % 2))


def flip_all(index, mask):
    distance = 1
    while distance <= mask:
        if mask & distance:
            index = flipped(index, distance)
        distance *= 2
    return index


def part_columns(width):
    tiles, count = width // LANES, len(ORDERS)
    edges = [tiles * p // count * LANES for p in range(count + 1)]
    return [(edges[p], edges[p + 1] - edges[p]) for p in range(count)]


def slot_of(part, mask):
    slot = 8 if mask & 1 else 0
    for place, bit in enumerate(ORDERS[part]):
        if mask >> bit & 1:
            slot |= 1 << place
    return slot


def moe_kernel(groups, columns, tok_ref, gain_ref, wg_ref, wu_ref, wd_ref, out_ref, *scratch):
    parts = len(columns)
    wgu, wd = scratch[:2]
    arrive = scratch[2 : 2 + parts]
    held = scratch[2 + parts : 2 + 2 * parts]
    sums = scratch[2 + 2 * parts : 2 + 3 * parts]
    taken = scratch[2 + 3 * parts : 2 + 4 * parts]
    final = scratch[2 + 4 * parts : 2 + 5 * parts]
    ended = scratch[2 + 5 * parts : 2 + 6 * parts]
    load_sem, send_sem, recv_sem = scratch[2 + 6 * parts :]
    me = lax.axis_index("ep")
    token_rows = tok_ref.shape[0]
    rows = groups * token_rows
    half = wg_ref.shape[1]

    loads = [
        pltpu.make_async_copy(wg_ref, wgu.at[:, 0:half], load_sem.at[0]),
        pltpu.make_async_copy(wu_ref, wgu.at[:, half : 2 * half], load_sem.at[1]),
        pltpu.make_async_copy(wd_ref, wd, load_sem.at[2]),
    ]
    for load in loads:
        load.start()

    partners = [1, 2, 4, 8] + [SPLIT * d for d in range(1, groups)]
    barrier = pltpu.get_barrier_semaphore()
    for mask in partners:
        pl.semaphore_signal(
            barrier, inc=1, device_id={"ep": flip_all(me, mask)}, device_id_type=MESH
        )
    pl.semaphore_wait(barrier, len(partners))

    counter = [0]

    def send(source, target, mask):
        number = counter[0]
        counter[0] += 1
        copy = pltpu.make_async_remote_copy(
            src_ref=source,
            dst_ref=target,
            send_sem=send_sem.at[number],
            recv_sem=recv_sem.at[number],
            device_id={"ep": flip_all(me, mask)},
            device_id_type=MESH,
        )
        copy.start()
        return copy

    everything = []

    first = []
    for p, (start, width) in enumerate(columns):
        first.append(
            [
                send(tok_ref.at[:, start : start + width], arrive[p].at[d], SPLIT * d)
                for d in range(1, groups)
            ]
        )

    across = [[] for _ in range(parts)]
    link = [None] * parts
    for p, (start, width) in enumerate(columns):
        for copy in first[p]:
            copy.wait_recv()
        pieces = [tok_ref[:, start : start + width].astype(jnp.float32)]
        pieces += [arrive[p][d].astype(jnp.float32) for d in range(1, groups)]
        held[p][0] = jnp.concatenate(pieces, axis=0).astype(jnp.bfloat16)
        link[p] = send(held[p].at[0:1], held[p].at[1:2], 1 << ORDERS[p][0])
        across[p].append(send(held[p].at[0:1], held[p].at[8:9], 1))
        everything += first[p]
    for stage in range(3):
        have = 1 << stage
        for p in range(parts):
            link[p].wait_recv()
            everything.append(link[p])
            if stage < 2:
                link[p] = send(
                    held[p].at[0 : 2 * have],
                    held[p].at[2 * have : 4 * have],
                    1 << ORDERS[p][stage + 1],
                )
            across[p].append(
                send(held[p].at[have : 2 * have], held[p].at[8 + have : 8 + 2 * have], 1)
            )

    loads[0].wait()
    loads[1].wait()
    act = None
    for p, (start, width) in enumerate(columns):
        for copy in across[p]:
            copy.wait_recv()
        everything += across[p]
        product = jnp.dot(
            held[p][...].reshape(SPLIT * rows, width),
            wgu[start : start + width, :],
            preferred_element_type=jnp.float32,
        )
        ordered = [None] * SPLIT
        for mask in range(SPLIT):
            slot = slot_of(p, mask)
            ordered[mask] = product[slot * rows : (slot + 1) * rows]
        product = jnp.concatenate(ordered, axis=0)
        act = product if act is None else act + product
    gate, up = act[:, 0:half], act[:, half : 2 * half]
    hidden = (gate / (1.0 + jnp.exp(-gate)) * up)
    loads[2].wait()

    across = [[] for _ in range(parts)]
    for p, (start, width) in enumerate(columns):
        ordered = [None] * SPLIT
        for mask in range(SPLIT):
            ordered[slot_of(p, mask)] = hidden[mask * rows : (mask + 1) * rows]
        mine = jnp.concatenate(ordered, axis=0).astype(jnp.bfloat16)
        down = wd[:, start : start + width]
        for low in (8, 0):
            sums[p][low : low + 8] = (
                jnp.dot(
                    mine[low * rows : (low + 8) * rows], down, preferred_element_type=jnp.float32
                )
                .astype(jnp.bfloat16)
                .reshape(8, rows, width)
            )
            if low:
                for a, b in ((12, 16), (10, 12), (8, 10)):
                    across[p].append(send(sums[p].at[a:b], taken[p].at[a:b], 1))

    def add(p, low, high, shift):
        total = sums[p][low:high].astype(jnp.float32)
        total += taken[p][low + shift : high + shift].astype(jnp.float32)
        sums[p][low:high] = total.astype(jnp.bfloat16)

    for p in range(parts):
        across[p][0].wait_recv()
        add(p, 4, 8, 8)
        link[p] = send(sums[p].at[4:8], taken[p].at[4:8], 1 << ORDERS[p][2])
    for p in range(parts):
        across[p][1].wait_recv()
        across[p][2].wait_recv()
        everything += across[p]
        add(p, 0, 4, 8)
    for stage in (1, 0):
        have = 1 << stage
        for p in range(parts):
            link[p].wait_recv()
            everything.append(link[p])
            add(p, have, 2 * have, 2 * have)
            link[p] = send(
                sums[p].at[have : 2 * have], taken[p].at[have : 2 * have], 1 << ORDERS[p][stage]
            )
        for p in range(parts):
            add(p, 0, have, 2 * have)

    last = []
    for p in range(parts):
        link[p].wait_recv()
        everything.append(link[p])
        total = sums[p][0].astype(jnp.float32) + taken[p][1].astype(jnp.float32)
        for d in range(groups):
            final[p][d] = total[d * token_rows : (d + 1) * token_rows].astype(jnp.bfloat16)
        last.append(
            [send(final[p].at[d], ended[p].at[d], SPLIT * d) for d in range(1, groups)]
        )
    for p, (start, width) in enumerate(columns):
        mixed = gain_ref[0][:, 0:1] * final[p][0].astype(jnp.float32)
        for d in range(1, groups):
            last[p][d - 1].wait_recv()
            mixed += gain_ref[d][:, 0:1] * ended[p][d].astype(jnp.float32)
        out_ref[:, start : start + width] = mixed.astype(jnp.bfloat16)
        everything += last[p]
    for copy in everything:
        copy.wait_send()


def experts(moe_in, expert_ids, expert_weights, w_gate, w_up, w_down):
    steps, token_count, width = moe_in.shape
    groups = lax.axis_size("ep") // SPLIT
    rows = steps * token_count
    my_group = lax.axis_index("ep") // SPLIT
    tokens = moe_in.reshape(rows, width)
    named = jnp.bitwise_xor(my_group, jnp.arange(groups, dtype=jnp.int32))
    ids = expert_ids.reshape(1, rows, -1)
    gains = jnp.sum(
        jnp.where(ids == named[:, None, None], expert_weights.reshape(1, rows, -1), 0.0), axis=2
    )
    gains = jnp.broadcast_to(gains[:, :, None], (groups, rows, LANES))
    columns = part_columns(width)
    hidden = w_gate.shape[1]
    slot_rows = groups * rows
    bf16 = jnp.bfloat16
    scratch = [pltpu.VMEM((width, 2 * hidden), bf16), pltpu.VMEM((hidden, width), bf16)]
    for shape in ((groups, rows), (SPLIT, slot_rows), (SPLIT, slot_rows), (SPLIT, slot_rows), (groups, rows), (groups, rows)):
        scratch += [pltpu.VMEM(shape + (wide,), bf16) for _, wide in columns]
    copies = len(columns) * (2 * (groups - 1) + 3 + 4 + 3 + 3)
    scratch += [pltpu.SemaphoreType.DMA((3,))] + [pltpu.SemaphoreType.DMA((copies,))] * 2
    vmem, anywhere = pl.BlockSpec(memory_space=pltpu.VMEM), pl.BlockSpec(memory_space=pl.ANY)
    out = pl.pallas_call(
        functools.partial(moe_kernel, groups, columns),
        out_shape=jax.ShapeDtypeStruct((rows, width), bf16),
        in_specs=[vmem, vmem, anywhere, anywhere, anywhere],
        out_specs=vmem,
        scratch_shapes=scratch,
        compiler_params=pltpu.CompilerParams(
            collective_id=0, has_side_effects=True, vmem_limit_bytes=48 * 2**20
        ),
        name="experts",
    )(tokens, gains, w_gate, w_up, w_down)
    return out.reshape(steps, token_count, width)


def attend_kernel(which_ref, len_ref, kv_ref, arr_ref, q_ref, new_ref, out_ref, cache_ref):
    r = pl.program_id(0)
    which, length = which_ref[r], len_ref[r]
    rows = kv_ref[0].astype(jnp.float32)
    for k in range(arr_ref.shape[0]):
        rows = jnp.where(which == k, arr_ref[k].astype(jnp.float32), rows)
    steps, heads, width = q_ref.shape[0], q_ref.shape[2], q_ref.shape[3]
    position = lax.broadcasted_iota(jnp.int32, rows.shape, 0)
    fresh = new_ref[0].astype(jnp.float32)
    for s in range(steps):
        rows = jnp.where(position == length + s, fresh[s : s + 1], rows)
    rows = rows.astype(jnp.bfloat16)
    cache_ref[0] = rows
    for s in range(steps):
        scores = (
            lax.dot_general(
                q_ref[s, 0], rows, (((1,), (1,)), ((), ())), preferred_element_type=jnp.float32
            )
            * softmax_scale
        )
        seen = lax.broadcasted_iota(jnp.int32, scores.shape, 1) < length + s + 1
        scores = jnp.where(seen, scores, jnp.float32(-1e30))
        weights = jnp.exp(scores - jnp.max(scores, axis=-1, keepdims=True))
        probabilities = (weights / jnp.sum(weights, axis=-1, keepdims=True)).astype(jnp.bfloat16)
        out_ref[s, 0] = jnp.dot(
            probabilities, rows[:, :LAT], preferred_element_type=jnp.float32
        ).astype(jnp.bfloat16)


def attend(kv_cache, arrivals, which, lengths, queries, new_latent):
    slots, positions, width = kv_cache.shape
    steps, _, heads, _ = queries.shape
    moves = arrivals.shape[0]
    grid = pltpu.PrefetchScalarGridSpec(
        num_scalar_prefetch=2,
        grid=(slots,),
        in_specs=[
            pl.BlockSpec((1, positions, width), lambda r, *_: (r, 0, 0)),
            pl.BlockSpec((moves, positions, width), lambda r, *_: (0, 0, 0)),
            pl.BlockSpec((steps, 1, heads, width), lambda r, *_: (0, r, 0, 0)),
            pl.BlockSpec((1, steps, width), lambda r, *_: (r, 0, 0)),
        ],
        out_specs=[
            pl.BlockSpec((steps, 1, heads, LAT), lambda r, *_: (0, r, 0, 0)),
            pl.BlockSpec((1, positions, width), lambda r, *_: (r, 0, 0)),
        ],
    )
    return pl.pallas_call(
        attend_kernel,
        grid_spec=grid,
        out_shape=[
            jax.ShapeDtypeStruct((steps, slots, heads, LAT), jnp.bfloat16),
            jax.ShapeDtypeStruct(kv_cache.shape, jnp.bfloat16),
        ],
        compiler_params=pltpu.CompilerParams(vmem_limit_bytes=32 * 2**20),
        name="attend",
    )(which, lengths, kv_cache, arrivals, queries, jnp.transpose(new_latent, (1, 0, 2)))


def exchange(payload, key):
    devices = lax.axis_size("ep")

    def by(mask):
        pairs = [(source, source ^ mask) for source in range(devices)]
        return lambda value: lax.ppermute(value, "ep", pairs)

    return lax.switch(key - 1, [by(mask) for mask in range(1, devices)], payload)


def migrate(kv_cache, cache_len, move_slot, move_key):
    devices = lax.axis_size("ep")
    my_index = lax.axis_index("ep")
    slot_count = kv_cache.shape[0]
    move_count = move_slot.shape[1]
    all_lengths = cache_len.reshape(devices, slot_count)
    my_lengths = lax.dynamic_index_in_dim(all_lengths, my_index, 0, keepdims=False)
    my_slots = lax.dynamic_index_in_dim(move_slot, my_index, 0, keepdims=False)
    arriving = []
    for k in range(move_count):
        payload = lax.dynamic_index_in_dim(kv_cache, my_slots[k], 0, keepdims=False)
        arriving.append(exchange(payload, move_key[k]))
    arrivals = jnp.stack(arriving)
    partners = jnp.bitwise_xor(my_index, move_key)
    source_slots = move_slot[partners, jnp.arange(move_count, dtype=jnp.int32)]
    arrival_lengths = all_lengths[partners, source_slots]
    slots = jnp.arange(slot_count, dtype=jnp.int32)
    which = jnp.full((slot_count,), -1, jnp.int32)
    lengths = my_lengths
    for k in range(move_count):
        which = jnp.where(slots == my_slots[k], k, which)
        lengths = jnp.where(slots == my_slots[k], arrival_lengths[k], lengths)
    return arrivals, which, lengths


def body(
    kv_cache,
    cache_len,
    move_slot,
    move_key,
    queries,
    new_latent,
    moe_in,
    expert_ids,
    expert_weights,
    w_gate,
    w_up,
    w_down,
):
    moe_out = experts(moe_in, expert_ids, expert_weights, w_gate, w_up, w_down)
    arrivals, which, lengths = migrate(kv_cache, cache_len, move_slot, move_key)
    attention_out, cache_out = attend(kv_cache, arrivals, which, lengths, queries, new_latent)
    return (attention_out, cache_out, moe_out)


def solution(mesh):
    in_specs = (
        P(("rep", "ep"), None, None),
        P("rep"),
        P("rep", None),
        P("rep"),
        P(None, ("rep", "ep"), None, None),
        P(None, ("rep", "ep"), None),
        P(None, ("rep", "ep"), None),
        P(None, ("rep", "ep"), None),
        P(None, ("rep", "ep"), None),
        P(None, "ep"),
        P(None, "ep"),
        P("ep", None),
    )
    out_specs = (
        P(None, ("rep", "ep"), None, None),
        P(("rep", "ep"), None, None),
        P(None, ("rep", "ep"), None),
    )
    return jax.shard_map(body, mesh=mesh, in_specs=in_specs, out_specs=out_specs, check_vma=False)
```

```python
import functools

import jax
import jax.numpy as jnp
from jax import lax
from jax.experimental import pallas as pl
from jax.experimental.pallas import tpu as pltpu
from jax.sharding import PartitionSpec as P

LAT = 512
SPLIT = 16
MESH = pl.DeviceIdType.MESH
LANES = 128
ORDERS = ((3, 1, 2), (3, 2, 1), (3, 1, 2), (3, 2, 1))

softmax_scale = 192.0 ** (-0.5)


def flipped(index, distance):
    return index + distance * (1 - 2 * ((index // distance) % 2))


def flip_all(index, mask):
    distance = 1
    while distance <= mask:
        if mask & distance:
            index = flipped(index, distance)
        distance *= 2
    return index


def part_columns(width):
    tiles, count = width // LANES, len(ORDERS)
    edges = [tiles * p // count * LANES for p in range(count + 1)]
    return [(edges[p], edges[p + 1] - edges[p]) for p in range(count)]


def slot_of(part, mask):
    slot = 8 if mask & 1 else 0
    for place, bit in enumerate(ORDERS[part]):
        if mask >> bit & 1:
            slot |= 1 << place
    return slot


def layer_kernel(groups, columns, orders, *refs):
    slot_ref, key_ref, id_ref, weight_ref, kv_ref, tok_ref, wg_ref, wu_ref, wd_ref = refs[:9]
    out_ref, arr_ref, outgoing, landed = refs[9:13]
    scratch = refs[13:]
    parts = len(columns)
    wgu, wd = scratch[:2]
    arrive = scratch[2 : 2 + parts]
    held = scratch[2 + parts : 2 + 2 * parts]
    sums = scratch[2 + 2 * parts : 2 + 3 * parts]
    taken = scratch[2 + 3 * parts : 2 + 4 * parts]
    final = scratch[2 + 4 * parts : 2 + 5 * parts]
    ended = scratch[2 + 5 * parts : 2 + 6 * parts]
    load_sem, send_sem, recv_sem = scratch[2 + 6 * parts :]
    me = lax.axis_index("ep")
    token_rows = tok_ref.shape[0]
    rows = groups * token_rows
    half = wg_ref.shape[1]

    loads = [
        pltpu.make_async_copy(wg_ref, wgu.at[:, 0:half], load_sem.at[0]),
        pltpu.make_async_copy(wu_ref, wgu.at[:, half : 2 * half], load_sem.at[1]),
        pltpu.make_async_copy(wd_ref, wd, load_sem.at[2]),
    ]
    for load in loads:
        load.start()

    partners = [1, 2, 4, 8] + [SPLIT * d for d in range(1, groups)]
    barrier = pltpu.get_barrier_semaphore()
    for mask in partners:
        pl.semaphore_signal(
            barrier, inc=1, device_id={"ep": flip_all(me, mask)}, device_id_type=MESH
        )
    pl.semaphore_wait(barrier, len(partners))

    counter = [0]

    def send(source, target, mask):
        number = counter[0]
        counter[0] += 1
        copy = pltpu.make_async_remote_copy(
            src_ref=source,
            dst_ref=target,
            send_sem=send_sem.at[number],
            recv_sem=recv_sem.at[number],
            device_id={"ep": flip_all(me, mask)},
            device_id_type=MESH,
        )
        copy.start()
        return copy

    everything = []

    moves, chunk = outgoing.shape[0], outgoing.shape[1] // len(orders)
    moving = [None] * len(orders)
    stage_of = [0] * len(orders)

    def part_of(c):
        return slice(c * chunk, (c + 1) * chunk)

    def depart(c):
        stage = stage_of[c]
        source = outgoing if stage == 0 else landed.at[stage - 1]
        moving[c] = send(
            source.at[:, part_of(c)], landed.at[stage, :, part_of(c)], 1 << orders[c][stage]
        )
        everything.append(moving[c])

    def advance():
        for c in range(len(orders)):
            moving[c].wait_recv()
            stage = stage_of[c]
            final_stage = stage == len(orders[c]) - 1
            for k in range(moves):
                other = landed[stage, k, part_of(c)]
                own = outgoing[k, part_of(c)] if stage == 0 else landed[stage - 1, k, part_of(c)]
                bit = (key_ref[k] // (1 << orders[c][stage])) % 2
                chosen = jnp.where(bit == 1, other, own)
                if final_stage:
                    arr_ref[k, part_of(c)] = chosen
                else:
                    landed[stage, k, part_of(c)] = chosen
            stage_of[c] += 1
            if not final_stage:
                depart(c)

    first = []
    for p, (start, width) in enumerate(columns):
        first.append(
            [
                send(tok_ref.at[:, start : start + width], arrive[p].at[d], SPLIT * d)
                for d in range(1, groups)
            ]
        )

    for k in range(moves):
        slot = slot_ref[me * moves + k]
        payload = kv_ref[0]
        for r in range(1, kv_ref.shape[0]):
            payload = jnp.where(slot == r, kv_ref[r], payload)
        outgoing[k] = payload
    for c in range(len(orders)):
        depart(c)

    across = [[] for _ in range(parts)]
    link = [None] * parts
    for p, (start, width) in enumerate(columns):
        for copy in first[p]:
            copy.wait_recv()
        pieces = [tok_ref[:, start : start + width].astype(jnp.float32)]
        pieces += [arrive[p][d].astype(jnp.float32) for d in range(1, groups)]
        held[p][0] = jnp.concatenate(pieces, axis=0).astype(jnp.bfloat16)
        link[p] = send(held[p].at[0:1], held[p].at[1:2], 1 << ORDERS[p][0])
        across[p].append(send(held[p].at[0:1], held[p].at[8:9], 1))
        everything += first[p]
    for stage in range(3):
        have = 1 << stage
        for p in range(parts):
            link[p].wait_recv()
            everything.append(link[p])
            if stage < 2:
                link[p] = send(
                    held[p].at[0 : 2 * have],
                    held[p].at[2 * have : 4 * have],
                    1 << ORDERS[p][stage + 1],
                )
            across[p].append(
                send(held[p].at[have : 2 * have], held[p].at[8 + have : 8 + 2 * have], 1)
            )
        if stage == 0:
            advance()

    loads[0].wait()
    loads[1].wait()
    act = None
    for p, (start, width) in enumerate(columns):
        for copy in across[p]:
            copy.wait_recv()
        everything += across[p]
        product = jnp.dot(
            held[p][...].reshape(SPLIT * rows, width),
            wgu[start : start + width, :],
            preferred_element_type=jnp.float32,
        )
        ordered = [None] * SPLIT
        for mask in range(SPLIT):
            slot = slot_of(p, mask)
            ordered[mask] = product[slot * rows : (slot + 1) * rows]
        product = jnp.concatenate(ordered, axis=0)
        act = product if act is None else act + product
    gate, up = act[:, 0:half], act[:, half : 2 * half]
    hidden = (gate / (1.0 + jnp.exp(-gate)) * up)
    loads[2].wait()

    across = [[] for _ in range(parts)]
    for p, (start, width) in enumerate(columns):
        ordered = [None] * SPLIT
        for mask in range(SPLIT):
            ordered[slot_of(p, mask)] = hidden[mask * rows : (mask + 1) * rows]
        mine = jnp.concatenate(ordered, axis=0).astype(jnp.bfloat16)
        down = wd[:, start : start + width]
        for low in (8, 0):
            sums[p][low : low + 8] = (
                jnp.dot(
                    mine[low * rows : (low + 8) * rows], down, preferred_element_type=jnp.float32
                )
                .astype(jnp.bfloat16)
                .reshape(8, rows, width)
            )
            if low:
                for a, b in ((12, 16), (10, 12), (8, 10)):
                    across[p].append(send(sums[p].at[a:b], taken[p].at[a:b], 1))

    def add(p, low, high, shift):
        total = sums[p][low:high].astype(jnp.float32)
        total += taken[p][low + shift : high + shift].astype(jnp.float32)
        sums[p][low:high] = total.astype(jnp.bfloat16)

    for p in range(parts):
        across[p][0].wait_recv()
        add(p, 4, 8, 8)
        link[p] = send(sums[p].at[4:8], taken[p].at[4:8], 1 << ORDERS[p][2])
    for p in range(parts):
        across[p][1].wait_recv()
        across[p][2].wait_recv()
        everything += across[p]
        add(p, 0, 4, 8)
    advance()
    for stage in (1, 0):
        have = 1 << stage
        for p in range(parts):
            link[p].wait_recv()
            everything.append(link[p])
            add(p, have, 2 * have, 2 * have)
            link[p] = send(
                sums[p].at[have : 2 * have], taken[p].at[have : 2 * have], 1 << ORDERS[p][stage]
            )
        for p in range(parts):
            add(p, 0, have, 2 * have)
        if stage == 1:
            advance()

    last = []
    for p in range(parts):
        link[p].wait_recv()
        everything.append(link[p])
        total = sums[p][0].astype(jnp.float32) + taken[p][1].astype(jnp.float32)
        for d in range(groups):
            final[p][d] = total[d * token_rows : (d + 1) * token_rows].astype(jnp.bfloat16)
        last.append(
            [send(final[p].at[d], ended[p].at[d], SPLIT * d) for d in range(1, groups)]
        )
    advance()
    tops = id_ref.shape[0] // token_rows
    row_of = lax.broadcasted_iota(jnp.int32, (token_rows, LANES), 0)
    gains = []
    for d in range(groups):
        expert = flip_all(me, SPLIT * d) // SPLIT
        gain = jnp.zeros((token_rows, LANES), jnp.float32)
        for row in range(token_rows):
            for top in range(tops):
                at = row * tops + top
                taken_here = jnp.where(id_ref[at] == expert, weight_ref[at], jnp.float32(0.0))
                gain = gain + jnp.where(row_of == row, taken_here, jnp.float32(0.0))
        gains.append(gain[:, 0:1])
    for p, (start, width) in enumerate(columns):
        mixed = gains[0] * final[p][0].astype(jnp.float32)
        for d in range(1, groups):
            last[p][d - 1].wait_recv()
            mixed += gains[d] * ended[p][d].astype(jnp.float32)
        out_ref[:, start : start + width] = mixed.astype(jnp.bfloat16)
        everything += last[p]
    while stage_of[0] < len(orders[0]):
        advance()
    for copy in everything:
        copy.wait_send()


def layer(slots_flat, move_key, kv, moe_in, expert_ids, expert_weights, w_gate, w_up, w_down):
    steps, token_count, width = moe_in.shape
    devices = lax.axis_size("ep")
    groups = devices // SPLIT
    rows = steps * token_count
    tokens = moe_in.reshape(rows, width)
    columns = part_columns(width)
    hidden = w_gate.shape[1]
    slot_rows = groups * rows
    moves = move_key.shape[0]
    high = list(range(4, devices.bit_length() - 1))
    orders = ([1] + high + [3, 2, 0], [2, 3] + high + [1, 0])
    bf16 = jnp.bfloat16
    payload = (moves,) + kv.shape[1:]
    scratch = [pltpu.VMEM(payload, bf16), pltpu.VMEM((len(orders[0]),) + payload, bf16)]
    scratch += [pltpu.VMEM((width, 2 * hidden), bf16), pltpu.VMEM((hidden, width), bf16)]
    outer, inner = (groups, rows), (SPLIT, slot_rows)
    for shape in (outer, inner, inner, inner, outer, outer):
        scratch += [pltpu.VMEM(shape + (wide,), bf16) for _, wide in columns]
    copies = len(columns) * (2 * (groups - 1) + 13) + len(orders) * len(orders[0])
    scratch += [pltpu.SemaphoreType.DMA((3,))] + [pltpu.SemaphoreType.DMA((copies,))] * 2
    vmem, anywhere = pl.BlockSpec(memory_space=pltpu.VMEM), pl.BlockSpec(memory_space=pl.ANY)
    smem = pl.BlockSpec(memory_space=pltpu.SMEM)
    out, arrivals = pl.pallas_call(
        functools.partial(layer_kernel, groups, columns, orders),
        out_shape=[
            jax.ShapeDtypeStruct((rows, width), bf16),
            jax.ShapeDtypeStruct(payload, bf16),
        ],
        in_specs=[smem] * 4 + [vmem, vmem, anywhere, anywhere, anywhere],
        out_specs=[vmem, vmem],
        scratch_shapes=scratch,
        compiler_params=pltpu.CompilerParams(
            collective_id=0, has_side_effects=True, vmem_limit_bytes=60 * 2**20
        ),
        name="layer",
    )(
        slots_flat,
        move_key,
        expert_ids.reshape(-1),
        expert_weights.reshape(-1),
        kv,
        tokens,
        w_gate,
        w_up,
        w_down,
    )
    return out.reshape(steps, token_count, width), arrivals


def attend_kernel(
    me_ref, slot_ref, key_ref, len_ref, kv_ref, arr_ref, q_ref, new_ref, out_ref, cache_ref
):
    r = pl.program_id(0)
    me, slots, moves = me_ref[0], pl.num_programs(0), arr_ref.shape[0]
    length = len_ref[me * slots + r]
    rows = kv_ref[0]
    for k in range(moves):
        here = slot_ref[me * moves + k] == r
        partner = me ^ key_ref[k]
        length = jnp.where(here, len_ref[partner * slots + slot_ref[partner * moves + k]], length)
        rows = jnp.where(here, arr_ref[k], rows)
    steps, heads = q_ref.shape[0], q_ref.shape[3]
    positions = rows.shape[1]
    step_of = lax.broadcasted_iota(jnp.int32, (steps, positions), 0)
    place = lax.broadcasted_iota(jnp.int32, (steps, positions), 1)
    spread = jnp.where(place == length + step_of, 1.0, 0.0).astype(jnp.bfloat16)
    fresh = lax.dot_general(
        new_ref[0], spread, (((0,), (0,)), ((), ())), preferred_element_type=jnp.float32
    )
    column = lax.broadcasted_iota(jnp.int32, rows.shape, 1)
    is_new = (column >= length) & (column < length + steps)
    rows = jnp.where(is_new, fresh, rows.astype(jnp.float32)).astype(jnp.bfloat16)
    cache_ref[0] = rows
    merged = jnp.concatenate([q_ref[s, 0] for s in range(steps)], axis=1)
    scores = (
        lax.dot_general(merged, rows, (((0,), (0,)), ((), ())), preferred_element_type=jnp.float32)
        * softmax_scale
    )
    at = lax.broadcasted_iota(jnp.int32, scores.shape, 1)
    step = lax.broadcasted_iota(jnp.int32, scores.shape, 0) // heads
    scores = jnp.where(at < length + step + 1, scores, jnp.float32(-1e30))
    weights = jnp.exp(scores - jnp.max(scores, axis=-1, keepdims=True))
    probabilities = (weights / jnp.sum(weights, axis=-1, keepdims=True)).astype(jnp.bfloat16)
    attended = lax.dot_general(
        probabilities, rows[:LAT], (((1,), (1,)), ((), ())), preferred_element_type=jnp.float32
    ).astype(jnp.bfloat16)
    for s in range(steps):
        out_ref[s, 0] = attended[s * heads : (s + 1) * heads]


def attend(me, slots_flat, move_key, cache_len, kv, arrivals, queries, new_latent):
    slots, width, positions = kv.shape
    steps, _, _, heads = queries.shape
    moves = arrivals.shape[0]
    grid = pltpu.PrefetchScalarGridSpec(
        num_scalar_prefetch=4,
        grid=(slots,),
        in_specs=[
            pl.BlockSpec((1, width, positions), lambda r, *_: (r, 0, 0)),
            pl.BlockSpec((moves, width, positions), lambda r, *_: (0, 0, 0)),
            pl.BlockSpec((steps, 1, width, heads), lambda r, *_: (0, r, 0, 0)),
            pl.BlockSpec((1, steps, width), lambda r, *_: (r, 0, 0)),
        ],
        out_specs=[
            pl.BlockSpec((steps, 1, heads, LAT), lambda r, *_: (0, r, 0, 0)),
            pl.BlockSpec((1, width, positions), lambda r, *_: (r, 0, 0)),
        ],
    )
    return pl.pallas_call(
        attend_kernel,
        grid_spec=grid,
        out_shape=[
            jax.ShapeDtypeStruct((steps, slots, heads, LAT), jnp.bfloat16),
            jax.ShapeDtypeStruct(kv.shape, jnp.bfloat16),
        ],
        compiler_params=pltpu.CompilerParams(vmem_limit_bytes=60 * 2**20),
        name="attend",
    )(
        me,
        slots_flat,
        move_key,
        cache_len,
        kv,
        arrivals,
        queries,
        jnp.transpose(new_latent, (1, 0, 2)),
    )


def body(
    kv_cache,
    cache_len,
    move_slot,
    move_key,
    queries,
    new_latent,
    moe_in,
    expert_ids,
    expert_weights,
    w_gate,
    w_up,
    w_down,
):
    me = lax.axis_index("ep").reshape(1)
    slots_flat = move_slot.reshape(-1)
    kv = jnp.transpose(kv_cache, (0, 2, 1))
    moe_out, arrivals = layer(
        slots_flat, move_key, kv, moe_in, expert_ids, expert_weights, w_gate, w_up, w_down
    )
    attention_out, cache = attend(
        me,
        slots_flat,
        move_key,
        cache_len,
        kv,
        arrivals,
        jnp.transpose(queries, (0, 1, 3, 2)),
        new_latent,
    )
    return (attention_out, jnp.transpose(cache, (0, 2, 1)), moe_out)


def solution(mesh):
    in_specs = (
        P(("rep", "ep"), None, None),
        P("rep"),
        P("rep", None),
        P("rep"),
        P(None, ("rep", "ep"), None, None),
        P(None, ("rep", "ep"), None),
        P(None, ("rep", "ep"), None),
        P(None, ("rep", "ep"), None),
        P(None, ("rep", "ep"), None),
        P(None, "ep"),
        P(None, "ep"),
        P("ep", None),
    )
    out_specs = (
        P(None, ("rep", "ep"), None, None),
        P(("rep", "ep"), None, None),
        P(None, ("rep", "ep"), None),
    )
    return jax.shard_map(body, mesh=mesh, in_specs=in_specs, out_specs=out_specs, check_vma=False)
```

```python
import functools

import jax
import jax.numpy as jnp
from jax import lax
from jax.experimental import pallas as pl
from jax.experimental.pallas import tpu as pltpu
from jax.sharding import PartitionSpec as P

LAT = 512
SPLIT = 16
MESH = pl.DeviceIdType.MESH
LANES = 128
ORDERS = ((3, 1, 2), (3, 2, 1)) * 3

softmax_scale = 192.0 ** (-0.5)


def flipped(index, distance):
    return index + distance * (1 - 2 * ((index // distance) % 2))


def flip_all(index, mask):
    distance = 1
    while distance <= mask:
        if mask & distance:
            index = flipped(index, distance)
        distance *= 2
    return index


def part_columns(width, tokens):
    wide, cuts = width // tokens, len(ORDERS) // (tokens - 1)
    edges = [wide // LANES * p // cuts * LANES for p in range(cuts + 1)]
    return [
        (section, edges[p], edges[p + 1] - edges[p]) for section in range(tokens - 1) for p in range(cuts)
    ]


def slot_of(part, mask):
    slot = 8 if mask & 1 else 0
    for place, bit in enumerate(ORDERS[part]):
        if mask >> bit & 1:
            slot |= 1 << place
    return slot


def layer_kernel(groups, columns, orders, *refs):
    slot_ref, key_ref, id_ref, weight_ref, kv_ref, tok_ref, wg_ref, wu_ref, wd_ref = refs[:9]
    out_ref, arr_ref, outgoing, landed = refs[9:13]
    scratch = refs[13:]
    parts = len(columns)
    wgu, wd = scratch[:2]
    packed, arrive, held, sums, taken, final, ended = [
        scratch[2 + n * parts : 2 + (n + 1) * parts] for n in range(7)
    ]
    load_sem, send_sem, recv_sem = scratch[2 + 7 * parts :]
    me = lax.axis_index("ep")
    steps, per_step, width = tok_ref.shape
    token_rows, tail = steps * per_step, width // per_step * (per_step - 1)
    rows = groups * token_rows
    half = wg_ref.shape[1]

    loads = [
        pltpu.make_async_copy(wg_ref, wgu.at[:, 0:half], load_sem.at[0]),
        pltpu.make_async_copy(wu_ref, wgu.at[:, half : 2 * half], load_sem.at[1]),
        pltpu.make_async_copy(wd_ref, wd, load_sem.at[2]),
    ]
    for load in loads:
        load.start()

    partners = [1, 2, 4, 8] + [SPLIT * d for d in range(1, groups)]
    barrier = pltpu.get_barrier_semaphore()
    for mask in partners:
        pl.semaphore_signal(
            barrier, inc=1, device_id={"ep": flip_all(me, mask)}, device_id_type=MESH
        )
    pl.semaphore_wait(barrier, len(partners))

    counter = [0]

    def send(source, target, mask):
        number = counter[0]
        counter[0] += 1
        copy = pltpu.make_async_remote_copy(
            src_ref=source,
            dst_ref=target,
            send_sem=send_sem.at[number],
            recv_sem=recv_sem.at[number],
            device_id={"ep": flip_all(me, mask)},
            device_id_type=MESH,
        )
        copy.start()
        return copy

    everything = []

    moves, chunk = outgoing.shape[0], outgoing.shape[1] // len(orders)
    moving = [None] * len(orders)
    stage_of = [0] * len(orders)

    def part_of(c):
        return slice(c * chunk, (c + 1) * chunk)

    def depart(c):
        stage = stage_of[c]
        source = outgoing if stage == 0 else landed.at[stage - 1]
        moving[c] = send(
            source.at[:, part_of(c)], landed.at[stage, :, part_of(c)], 1 << orders[c][stage]
        )
        everything.append(moving[c])

    def advance():
        for c in range(len(orders)):
            moving[c].wait_recv()
            stage = stage_of[c]
            final_stage = stage == len(orders[c]) - 1
            for k in range(moves):
                other = landed[stage, k, part_of(c)]
                own = outgoing[k, part_of(c)] if stage == 0 else landed[stage - 1, k, part_of(c)]
                bit = (key_ref[k] // (1 << orders[c][stage])) % 2
                chosen = jnp.where(bit == 1, other, own)
                if final_stage:
                    arr_ref[k, part_of(c)] = chosen
                else:
                    landed[stage, k, part_of(c)] = chosen
            stage_of[c] += 1
            if not final_stage:
                depart(c)

    rank, gain = [], []
    for d in range(groups):
        expert = flip_all(me, SPLIT * d) // SPLIT
        rank.append([])
        gain.append([])
        for s in range(steps):
            seen = 0
            for t in range(per_step):
                named, weight = 0, jnp.float32(0.0)
                for top in range(id_ref.shape[1]):
                    match = id_ref[s, top, t] == expert
                    named = named + jnp.where(match, 1, 0)
                    weight = weight + jnp.where(match, weight_ref[s, top, t], jnp.float32(0.0))
                rank[d].append(jnp.where(named > 0, seen, -1))
                gain[d].append(weight)
                seen = seen + named

    def chosen_rows(d, section, transposed):
        shape = (token_rows, token_rows)
        packed_row = lax.broadcasted_iota(jnp.int32, shape, 1 if transposed else 0)
        token_row = lax.broadcasted_iota(jnp.int32, shape, 0 if transposed else 1)
        main = jnp.zeros(shape, jnp.float32)
        last = jnp.zeros(shape, jnp.float32)
        for row in range(token_rows):
            base = row // per_step * per_step
            place = rank[d][row]
            at_main = jnp.where(place >= 0, base + place, -1)
            at_last = jnp.where(place == section, base + per_step - 1, -1)
            main += jnp.where((token_row == row) & (packed_row == at_main), 1.0, 0.0)
            last += jnp.where((token_row == row) & (packed_row == at_last), 1.0, 0.0)
        return main, last

    tokens = jnp.concatenate([tok_ref[s].astype(jnp.float32) for s in range(steps)], axis=0)

    def pack(d, section, start, low, wide):
        main, last = chosen_rows(d, section, False)
        matrix = jnp.concatenate([main, last], axis=1).astype(jnp.bfloat16)
        both = jnp.concatenate(
            [tokens[:, start : start + wide], tokens[:, low : low + wide]], axis=0
        ).astype(jnp.bfloat16)
        return jnp.dot(matrix, both, preferred_element_type=jnp.float32)

    place_of = []
    for section, offset, wide in columns:
        place_of.append((section, section * (width // per_step) + offset, tail + offset, wide))

    first = []
    for p, place in enumerate(place_of):
        first.append([])
        for d in range(1, groups):
            packed[p][d] = pack(d, *place).astype(jnp.bfloat16)
            first[p].append(send(packed[p].at[d], arrive[p].at[d], SPLIT * d))

    for k in range(moves):
        slot = slot_ref[k, me]
        payload = kv_ref[0]
        for r in range(1, kv_ref.shape[0]):
            payload = jnp.where(slot == r, kv_ref[r], payload)
        outgoing[k] = payload
    for c in range(len(orders)):
        depart(c)

    across = [[] for _ in range(parts)]
    link = [None] * parts
    for p, place in enumerate(place_of):
        mine = pack(0, *place)
        for copy in first[p]:
            copy.wait_recv()
        pieces = [mine]
        pieces += [arrive[p][d].astype(jnp.float32) for d in range(1, groups)]
        held[p][0] = jnp.concatenate(pieces, axis=0).astype(jnp.bfloat16)
        link[p] = send(held[p].at[0:1], held[p].at[1:2], 1 << ORDERS[p][0])
        across[p].append(send(held[p].at[0:1], held[p].at[8:9], 1))
        everything += first[p]
    for stage in range(3):
        have = 1 << stage
        for p in range(parts):
            link[p].wait_recv()
            everything.append(link[p])
            if stage < 2:
                link[p] = send(
                    held[p].at[0 : 2 * have],
                    held[p].at[2 * have : 4 * have],
                    1 << ORDERS[p][stage + 1],
                )
            across[p].append(
                send(held[p].at[have : 2 * have], held[p].at[8 + have : 8 + 2 * have], 1)
            )
        if stage == 0:
            advance()

    loads[0].wait()
    loads[1].wait()
    act = None
    in_step = lax.broadcasted_iota(jnp.int32, (SPLIT * rows, 2 * half), 0) % per_step
    for p, (section, start, low, wide) in enumerate(place_of):
        for copy in across[p]:
            copy.wait_recv()
        everything += across[p]
        block = held[p][...].reshape(SPLIT * rows, wide)
        product = jnp.dot(block, wgu[start : start + wide, :], preferred_element_type=jnp.float32)
        ends = jnp.dot(block, wgu[low : low + wide, :], preferred_element_type=jnp.float32)
        shift = per_step - 1 - section
        ends = jnp.concatenate([ends[shift:], ends[:shift]], axis=0)
        product += jnp.where(in_step == section, ends, 0.0)
        ordered = [None] * SPLIT
        for mask in range(SPLIT):
            slot = slot_of(p, mask)
            ordered[mask] = product[slot * rows : (slot + 1) * rows]
        product = jnp.concatenate(ordered, axis=0)
        act = product if act is None else act + product
    gate, up = act[:, 0:half], act[:, half : 2 * half]
    hidden = (gate / (1.0 + jnp.exp(-gate)) * up)
    loads[2].wait()

    across = [[] for _ in range(parts)]
    in_step = in_step[:, 0:half]
    hidden = jnp.where(in_step == per_step - 1, 0.0, hidden)
    for p, (section, start, low, wide) in enumerate(place_of):
        shift = per_step - 1 - section
        moved = jnp.concatenate([hidden[-shift:], hidden[:-shift]], axis=0)
        moved = jnp.where(in_step == per_step - 1, moved, 0.0)
        both = jnp.concatenate([hidden, moved], axis=1)
        ordered = [None] * SPLIT
        for mask in range(SPLIT):
            ordered[slot_of(p, mask)] = both[mask * rows : (mask + 1) * rows]
        mine = jnp.concatenate(ordered, axis=0).astype(jnp.bfloat16)
        down = jnp.concatenate([wd[:, start : start + wide], wd[:, low : low + wide]], axis=0)
        for low in (8, 0):
            sums[p][low : low + 8] = (
                jnp.dot(
                    mine[low * rows : (low + 8) * rows], down, preferred_element_type=jnp.float32
                )
                .astype(jnp.bfloat16)
                .reshape(8, rows, wide)
            )
            if low:
                for a, b in ((12, 16), (10, 12), (8, 10)):
                    across[p].append(send(sums[p].at[a:b], taken[p].at[a:b], 1))

    def add(p, low, high, shift):
        total = sums[p][low:high].astype(jnp.float32)
        total += taken[p][low + shift : high + shift].astype(jnp.float32)
        sums[p][low:high] = total.astype(jnp.bfloat16)

    for p in range(parts):
        across[p][0].wait_recv()
        add(p, 4, 8, 8)
        link[p] = send(sums[p].at[4:8], taken[p].at[4:8], 1 << ORDERS[p][2])
    for p in range(parts):
        across[p][1].wait_recv()
        across[p][2].wait_recv()
        everything += across[p]
        add(p, 0, 4, 8)
    advance()
    for stage in (1, 0):
        have = 1 << stage
        for p in range(parts):
            link[p].wait_recv()
            everything.append(link[p])
            add(p, have, 2 * have, 2 * have)
            link[p] = send(
                sums[p].at[have : 2 * have], taken[p].at[have : 2 * have], 1 << ORDERS[p][stage]
            )
        for p in range(parts):
            add(p, 0, have, 2 * have)
        if stage == 1:
            advance()

    last = []
    for p in range(parts):
        link[p].wait_recv()
        everything.append(link[p])
        total = sums[p][0].astype(jnp.float32) + taken[p][1].astype(jnp.float32)
        for d in range(groups):
            final[p][d] = total[d * token_rows : (d + 1) * token_rows].astype(jnp.bfloat16)
        last.append(
            [send(final[p].at[d], ended[p].at[d], SPLIT * d) for d in range(1, groups)]
        )
    advance()
    row_of = lax.broadcasted_iota(jnp.int32, (token_rows, LANES), 0)
    gains = []
    for d in range(groups):
        column = jnp.zeros((token_rows, LANES), jnp.float32)
        for row in range(token_rows):
            column += jnp.where(row_of == row, gain[d][row], jnp.float32(0.0))
        gains.append(column[:, 0:1])
    ends = {}
    for p, (section, start, low, wide) in enumerate(place_of):
        mixed = None
        for d in range(groups):
            if d:
                last[p][d - 1].wait_recv()
            home = ended[p][d] if d else final[p][0]
            main, tails = chosen_rows(d, section, True)
            matrix = jnp.concatenate([main, tails], axis=0).astype(jnp.bfloat16)
            unpacked = jnp.dot(matrix, home, preferred_element_type=jnp.float32)
            unpacked = unpacked * jnp.concatenate([gains[d], gains[d]], axis=0)
            mixed = unpacked if mixed is None else mixed + unpacked
        for s in range(steps):
            out_ref[s, :, start : start + wide] = mixed[
                s * per_step : (s + 1) * per_step
            ].astype(jnp.bfloat16)
        after = mixed[token_rows:]
        ends[low] = (ends[low][0] + after, wide) if low in ends else (after, wide)
        everything += last[p]
    for low, (mixed, wide) in ends.items():
        for s in range(steps):
            out_ref[s, :, low : low + wide] = mixed[s * per_step : (s + 1) * per_step].astype(
                jnp.bfloat16
            )
    while stage_of[0] < len(orders[0]):
        advance()
    for copy in everything:
        copy.wait_send()


def layer(slot_table, move_key, kv, moe_in, expert_ids, expert_weights, w_gate, w_up, w_down):
    steps, token_count, width = moe_in.shape
    devices = lax.axis_size("ep")
    groups = devices // SPLIT
    rows = steps * token_count
    columns = part_columns(width, token_count)
    hidden = w_gate.shape[1]
    slot_rows = groups * rows
    moves = move_key.shape[0]
    high = list(range(4, devices.bit_length() - 1))
    orders = ([1] + high + [3, 2, 0], [2, 3] + high + [1, 0])
    bf16 = jnp.bfloat16
    payload = (moves,) + kv.shape[1:]
    scratch = [pltpu.VMEM(payload, bf16), pltpu.VMEM((len(orders[0]),) + payload, bf16)]
    scratch += [pltpu.VMEM((width, 2 * hidden), bf16), pltpu.VMEM((hidden, width), bf16)]
    outer, inner = (groups, rows), (SPLIT, slot_rows)
    for shape in (outer, outer, inner, inner, inner, outer, outer):
        scratch += [pltpu.VMEM(shape + (wide,), bf16) for _, _, wide in columns]
    copies = len(columns) * (2 * (groups - 1) + 13) + len(orders) * len(orders[0])
    scratch += [pltpu.SemaphoreType.DMA((3,))] + [pltpu.SemaphoreType.DMA((copies,))] * 2
    vmem, anywhere = pl.BlockSpec(memory_space=pltpu.VMEM), pl.BlockSpec(memory_space=pl.ANY)
    smem = pl.BlockSpec(memory_space=pltpu.SMEM)
    out, arrivals = pl.pallas_call(
        functools.partial(layer_kernel, groups, columns, orders),
        out_shape=[
            jax.ShapeDtypeStruct(moe_in.shape, bf16),
            jax.ShapeDtypeStruct(payload, bf16),
        ],
        in_specs=[smem] * 4 + [vmem, vmem, anywhere, anywhere, anywhere],
        out_specs=[vmem, vmem],
        scratch_shapes=scratch,
        compiler_params=pltpu.CompilerParams(
            collective_id=0, has_side_effects=True, vmem_limit_bytes=60 * 2**20
        ),
        name="layer",
    )(
        slot_table,
        move_key,
        jnp.transpose(expert_ids, (0, 2, 1)),
        jnp.transpose(expert_weights, (0, 2, 1)),
        kv,
        moe_in,
        w_gate,
        w_up,
        w_down,
    )
    return out, arrivals


def attend_kernel(
    me_ref, slot_ref, key_ref, len_ref, kv_ref, arr_ref, q_ref, new_ref, out_ref, cache_ref
):
    r = pl.program_id(0)
    me, slots, moves = me_ref[0], pl.num_programs(0), arr_ref.shape[0]
    length = len_ref[me * slots + r]
    rows = kv_ref[0]
    for k in range(moves):
        here = slot_ref[k, me] == r
        partner = me ^ key_ref[k]
        length = jnp.where(here, len_ref[partner * slots + slot_ref[k, partner]], length)
        rows = jnp.where(here, arr_ref[k], rows)
    steps, heads = q_ref.shape[0], q_ref.shape[3]
    positions = rows.shape[1]
    owner = lax.broadcasted_iota(jnp.int32, (new_ref.shape[1], positions), 0)
    place = lax.broadcasted_iota(jnp.int32, (new_ref.shape[1], positions), 1)
    fresh = None
    for s in range(steps):
        spread = jnp.where((owner == r) & (place == length + s), 1.0, 0.0).astype(jnp.bfloat16)
        piece = lax.dot_general(
            new_ref[s], spread, (((0,), (0,)), ((), ())), preferred_element_type=jnp.float32
        )
        fresh = piece if fresh is None else fresh + piece
    column = lax.broadcasted_iota(jnp.int32, rows.shape, 1)
    is_new = (column >= length) & (column < length + steps)
    rows = jnp.where(is_new, fresh, rows.astype(jnp.float32)).astype(jnp.bfloat16)
    cache_ref[0] = rows
    merged = jnp.concatenate([q_ref[s, 0] for s in range(steps)], axis=1)
    scores = (
        lax.dot_general(merged, rows, (((0,), (0,)), ((), ())), preferred_element_type=jnp.float32)
        * softmax_scale
    )
    at = lax.broadcasted_iota(jnp.int32, scores.shape, 1)
    step = lax.broadcasted_iota(jnp.int32, scores.shape, 0) // heads
    scores = jnp.where(at < length + step + 1, scores, jnp.float32(-1e30))
    weights = jnp.exp(scores - jnp.max(scores, axis=-1, keepdims=True))
    probabilities = (weights / jnp.sum(weights, axis=-1, keepdims=True)).astype(jnp.bfloat16)
    attended = lax.dot_general(
        probabilities, rows[:LAT], (((1,), (1,)), ((), ())), preferred_element_type=jnp.float32
    ).astype(jnp.bfloat16)
    for s in range(steps):
        out_ref[s, 0] = attended[s * heads : (s + 1) * heads]


def attend(me, slot_table, move_key, cache_len, kv, arrivals, queries, new_latent):
    slots, width, positions = kv.shape
    steps, _, _, heads = queries.shape
    moves = arrivals.shape[0]
    grid = pltpu.PrefetchScalarGridSpec(
        num_scalar_prefetch=4,
        grid=(slots,),
        in_specs=[
            pl.BlockSpec((1, width, positions), lambda r, *_: (r, 0, 0)),
            pl.BlockSpec((moves, width, positions), lambda r, *_: (0, 0, 0)),
            pl.BlockSpec((steps, 1, width, heads), lambda r, *_: (0, r, 0, 0)),
            pl.BlockSpec(new_latent.shape, lambda r, *_: (0, 0, 0)),
        ],
        out_specs=[
            pl.BlockSpec((steps, 1, heads, LAT), lambda r, *_: (0, r, 0, 0)),
            pl.BlockSpec((1, width, positions), lambda r, *_: (r, 0, 0)),
        ],
    )
    return pl.pallas_call(
        attend_kernel,
        grid_spec=grid,
        out_shape=[
            jax.ShapeDtypeStruct((steps, slots, heads, LAT), jnp.bfloat16),
            jax.ShapeDtypeStruct(kv.shape, jnp.bfloat16),
        ],
        compiler_params=pltpu.CompilerParams(vmem_limit_bytes=60 * 2**20),
        name="attend",
    )(
        me,
        slot_table,
        move_key,
        cache_len,
        kv,
        arrivals,
        queries,
        new_latent,
    )


def body(
    kv_cache,
    cache_len,
    move_slot,
    move_key,
    queries,
    new_latent,
    moe_in,
    expert_ids,
    expert_weights,
    w_gate,
    w_up,
    w_down,
):
    me = lax.axis_index("ep").reshape(1)
    slot_table = jnp.transpose(move_slot)
    kv = jnp.transpose(kv_cache, (0, 2, 1))
    moe_out, arrivals = layer(
        slot_table, move_key, kv, moe_in, expert_ids, expert_weights, w_gate, w_up, w_down
    )
    attention_out, cache = attend(
        me,
        slot_table,
        move_key,
        cache_len,
        kv,
        arrivals,
        jnp.transpose(queries, (0, 1, 3, 2)),
        new_latent,
    )
    return (attention_out, jnp.transpose(cache, (0, 2, 1)), moe_out)


def solution(mesh):
    in_specs = (
        P(("rep", "ep"), None, None),
        P("rep"),
        P("rep", None),
        P("rep"),
        P(None, ("rep", "ep"), None, None),
        P(None, ("rep", "ep"), None),
        P(None, ("rep", "ep"), None),
        P(None, ("rep", "ep"), None),
        P(None, ("rep", "ep"), None),
        P(None, "ep"),
        P(None, "ep"),
        P("ep", None),
    )
    out_specs = (
        P(None, ("rep", "ep"), None, None),
        P(("rep", "ep"), None, None),
        P(None, ("rep", "ep"), None),
    )
    return jax.shard_map(body, mesh=mesh, in_specs=in_specs, out_specs=out_specs, check_vma=False)
```

```python
import functools

import jax
import jax.numpy as jnp
from jax import lax
from jax.experimental import pallas as pl
from jax.experimental.pallas import tpu as pltpu
from jax.sharding import PartitionSpec as P

LAT = 512
SPLIT = 16
MESH = pl.DeviceIdType.MESH
LANES = 128
ORDERS = ((3, 1, 2), (3, 2, 1)) * 3
softmax_scale = 192.0 ** (-0.5)


def flipped(index, distance):
    return index + distance * (1 - 2 * ((index // distance) % 2))


def flip_all(index, mask):
    distance = 1
    while distance <= mask:
        if mask & distance:
            index = flipped(index, distance)
        distance *= 2
    return index


def part_columns(width, tokens):
    wide, cuts = width // tokens, len(ORDERS) // (tokens - 1)
    edges = [wide // LANES * p // cuts * LANES for p in range(cuts + 1)]
    return [
        (section, edges[p], edges[p + 1] - edges[p]) for section in range(tokens - 1) for p in range(cuts)
    ]


def slot_of(part, mask):
    slot = 8 if mask & 1 else 0
    for place, bit in enumerate(ORDERS[part]):
        if mask >> bit & 1:
            slot |= 1 << place
    return slot


def in_steps(parts, stages):
    return [(p, stage) for stage in range(stages) for p in range(parts)]


def layer_kernel(groups, columns, orders, *refs):
    slot_ref, key_ref, id_ref, weight_ref, kv_ref, tok_ref, wg_ref, wu_ref, wd_ref = refs[:9]
    out_ref, arr_ref, outgoing, landed = refs[9:13]
    scratch = refs[13:]
    parts = len(columns)
    wgu, wd = scratch[:2]
    packed, arrive, held, sums, taken, final, ended = [
        scratch[2 + n * parts : 2 + (n + 1) * parts] for n in range(7)
    ]
    load_sem, send_sem, recv_sem = scratch[2 + 7 * parts :]
    me = lax.axis_index("ep")
    steps, per_step, width = tok_ref.shape
    token_rows, tail = steps * per_step, width // per_step * (per_step - 1)
    rows = groups * token_rows
    half = wg_ref.shape[1]

    loads = [
        pltpu.make_async_copy(wg_ref, wgu.at[:, 0:half], load_sem.at[0]),
        pltpu.make_async_copy(wu_ref, wgu.at[:, half : 2 * half], load_sem.at[1]),
        pltpu.make_async_copy(wd_ref, wd, load_sem.at[2]),
    ]
    for load in loads:
        load.start()

    partners = [1, 2, 4, 8] + [SPLIT * d for d in range(1, groups)]
    barrier = pltpu.get_barrier_semaphore()
    for mask in partners:
        pl.semaphore_signal(
            barrier, inc=1, device_id={"ep": flip_all(me, mask)}, device_id_type=MESH
        )
    pl.semaphore_wait(barrier, len(partners))

    counter = [0]

    def send(source, target, mask):
        number = counter[0]
        counter[0] += 1
        copy = pltpu.make_async_remote_copy(
            src_ref=source,
            dst_ref=target,
            send_sem=send_sem.at[number],
            recv_sem=recv_sem.at[number],
            device_id={"ep": flip_all(me, mask)},
            device_id_type=MESH,
        )
        copy.start()
        return copy

    everything = []

    moves, chunk = outgoing.shape[0], outgoing.shape[1] // len(orders)
    moving = [None] * len(orders)
    stage_of = [0] * len(orders)

    def part_of(c):
        return slice(c * chunk, (c + 1) * chunk)

    def depart(c):
        stage = stage_of[c]
        source = outgoing if stage == 0 else landed.at[stage - 1]
        moving[c] = send(
            source.at[:, part_of(c)], landed.at[stage, :, part_of(c)], 1 << orders[c][stage]
        )
        everything.append(moving[c])

    def advance():
        for c in range(len(orders)):
            moving[c].wait_recv()
            stage = stage_of[c]
            final_stage = stage == len(orders[c]) - 1
            for k in range(moves):
                other = landed[stage, k, part_of(c)]
                own = outgoing[k, part_of(c)] if stage == 0 else landed[stage - 1, k, part_of(c)]
                bit = (key_ref[k] // (1 << orders[c][stage])) % 2
                chosen = jnp.where(bit == 1, other, own)
                if final_stage:
                    arr_ref[k, part_of(c)] = chosen
                else:
                    landed[stage, k, part_of(c)] = chosen
            stage_of[c] += 1
            if not final_stage:
                depart(c)

    rank, gain = [], []
    for d in range(groups):
        expert = flip_all(me, SPLIT * d) // SPLIT
        rank.append([])
        gain.append([])
        for s in range(steps):
            seen = 0
            for t in range(per_step):
                named, weight = 0, jnp.float32(0.0)
                for top in range(id_ref.shape[1]):
                    match = id_ref[s, top, t] == expert
                    named = named + jnp.where(match, 1, 0)
                    weight = weight + jnp.where(match, weight_ref[s, top, t], jnp.float32(0.0))
                rank[d].append(jnp.where(named > 0, seen, -1))
                gain[d].append(weight)
                seen = seen + named

    def chosen_rows(d, section, transposed):
        shape = (token_rows, token_rows)
        packed_row = lax.broadcasted_iota(jnp.int32, shape, 1 if transposed else 0)
        token_row = lax.broadcasted_iota(jnp.int32, shape, 0 if transposed else 1)
        main = jnp.zeros(shape, jnp.float32)
        last = jnp.zeros(shape, jnp.float32)
        for row in range(token_rows):
            base = row // per_step * per_step
            place = rank[d][row]
            at_main = jnp.where(place >= 0, base + place, -1)
            at_last = jnp.where(place == section, base + per_step - 1, -1)
            main += jnp.where((token_row == row) & (packed_row == at_main), 1.0, 0.0)
            last += jnp.where((token_row == row) & (packed_row == at_last), 1.0, 0.0)
        return main, last

    tokens = jnp.concatenate([tok_ref[s].astype(jnp.float32) for s in range(steps)], axis=0)

    def pack(d, section, start, low, wide):
        main, last = chosen_rows(d, section, False)
        matrix = jnp.concatenate([main, last], axis=1).astype(jnp.bfloat16)
        both = jnp.concatenate(
            [tokens[:, start : start + wide], tokens[:, low : low + wide]], axis=0
        ).astype(jnp.bfloat16)
        return jnp.dot(matrix, both, preferred_element_type=jnp.float32)

    place_of = []
    for section, offset, wide in columns:
        place_of.append((section, section * (width // per_step) + offset, tail + offset, wide))

    first = []
    for p, place in enumerate(place_of):
        first.append([])
        for d in range(1, groups):
            packed[p][d] = pack(d, *place).astype(jnp.bfloat16)
            first[p].append(send(packed[p].at[d], arrive[p].at[d], SPLIT * d))

    for k in range(moves):
        slot = slot_ref[k, me]
        payload = kv_ref[0]
        for r in range(1, kv_ref.shape[0]):
            payload = jnp.where(slot == r, kv_ref[r], payload)
        outgoing[k] = payload
    for c in range(len(orders)):
        depart(c)

    across = [[] for _ in range(parts)]
    link = [None] * parts
    for p, stage in in_steps(parts, 4):
        if stage == 0:
            mine = pack(0, *place_of[p])
            for copy in first[p]:
                copy.wait_recv()
            everything += first[p]
            pieces = [mine]
            pieces += [arrive[p][d].astype(jnp.float32) for d in range(1, groups)]
            held[p][0] = jnp.concatenate(pieces, axis=0).astype(jnp.bfloat16)
        else:
            link[p].wait_recv()
            everything.append(link[p])
        have = 1 << stage
        if stage < 3:
            link[p] = send(
                held[p].at[0:have], held[p].at[have : 2 * have], 1 << ORDERS[p][stage]
            )
        low = have // 2
        across[p].append(send(held[p].at[low:have], held[p].at[8 + low : 8 + have], 1))
        if (p, stage) == (parts - 1, 1):
            advance()

    loads[0].wait()
    loads[1].wait()
    act = None
    in_step = lax.broadcasted_iota(jnp.int32, (SPLIT * rows, 2 * half), 0) % per_step
    for p, (section, start, low, wide) in enumerate(place_of):
        for copy in across[p]:
            copy.wait_recv()
        everything += across[p]
        block = held[p][...].reshape(SPLIT * rows, wide)
        product = jnp.dot(block, wgu[start : start + wide, :], preferred_element_type=jnp.float32)
        ends = jnp.dot(block, wgu[low : low + wide, :], preferred_element_type=jnp.float32)
        shift = per_step - 1 - section
        ends = jnp.concatenate([ends[shift:], ends[:shift]], axis=0)
        product += jnp.where(in_step == section, ends, 0.0)
        ordered = [None] * SPLIT
        for mask in range(SPLIT):
            slot = slot_of(p, mask)
            ordered[mask] = product[slot * rows : (slot + 1) * rows]
        product = jnp.concatenate(ordered, axis=0)
        act = product if act is None else act + product
    gate, up = act[:, 0:half], act[:, half : 2 * half]
    hidden = (gate / (1.0 + jnp.exp(-gate)) * up)
    loads[2].wait()

    across = [[] for _ in range(parts)]
    in_step = in_step[:, 0:half]
    hidden = jnp.where(in_step == per_step - 1, 0.0, hidden)
    for p, (section, start, low, wide) in enumerate(place_of):
        shift = per_step - 1 - section
        moved = jnp.concatenate([hidden[-shift:], hidden[:-shift]], axis=0)
        moved = jnp.where(in_step == per_step - 1, moved, 0.0)
        both = jnp.concatenate([hidden, moved], axis=1)
        ordered = [None] * SPLIT
        for mask in range(SPLIT):
            ordered[slot_of(p, mask)] = both[mask * rows : (mask + 1) * rows]
        mine = jnp.concatenate(ordered, axis=0).astype(jnp.bfloat16)
        down = jnp.concatenate([wd[:, start : start + wide], wd[:, low : low + wide]], axis=0)
        for low in (8, 0):
            sums[p][low : low + 8] = (
                jnp.dot(
                    mine[low * rows : (low + 8) * rows], down, preferred_element_type=jnp.float32
                )
                .astype(jnp.bfloat16)
                .reshape(8, rows, wide)
            )
            if low:
                for a, b in ((12, 16), (10, 12), (8, 10)):
                    across[p].append(send(sums[p].at[a:b], taken[p].at[a:b], 1))

    def add(p, low, high, shift):
        sums[p][low:high] = sums[p][low:high] + taken[p][low + shift : high + shift]

    last = [None] * parts
    for p, stage in in_steps(parts, 4):
        if stage == 0:
            across[p][0].wait_recv()
            add(p, 4, 8, 8)
            link[p] = send(sums[p].at[4:8], taken[p].at[4:8], 1 << ORDERS[p][2])
            across[p][1].wait_recv()
            across[p][2].wait_recv()
            everything += across[p]
            add(p, 0, 4, 8)
        elif stage < 3:
            have = 4 >> stage
            link[p].wait_recv()
            everything.append(link[p])
            add(p, have, 2 * have, 2 * have)
            link[p] = send(
                sums[p].at[have : 2 * have],
                taken[p].at[have : 2 * have],
                1 << ORDERS[p][2 - stage],
            )
            add(p, 0, have, 2 * have)
        else:
            link[p].wait_recv()
            everything.append(link[p])
            total = sums[p][0].astype(jnp.float32) + taken[p][1].astype(jnp.float32)
            for d in range(groups):
                final[p][d] = total[d * token_rows : (d + 1) * token_rows].astype(jnp.bfloat16)
            last[p] = [send(final[p].at[d], ended[p].at[d], SPLIT * d) for d in range(1, groups)]
        if p == parts - 1 and stage != 2:
            advance()
    row_of = lax.broadcasted_iota(jnp.int32, (token_rows, LANES), 0)
    gains = []
    for d in range(groups):
        column = jnp.zeros((token_rows, LANES), jnp.float32)
        for row in range(token_rows):
            column += jnp.where(row_of == row, gain[d][row], jnp.float32(0.0))
        gains.append(column[:, 0:1])
    ends = {}
    for p, (section, start, low, wide) in enumerate(place_of):
        mixed = None
        for d in range(groups):
            if d:
                last[p][d - 1].wait_recv()
            home = ended[p][d] if d else final[p][0]
            main, tails = chosen_rows(d, section, True)
            matrix = jnp.concatenate([main, tails], axis=0).astype(jnp.bfloat16)
            unpacked = jnp.dot(matrix, home, preferred_element_type=jnp.float32)
            unpacked = unpacked * jnp.concatenate([gains[d], gains[d]], axis=0)
            mixed = unpacked if mixed is None else mixed + unpacked
        for s in range(steps):
            out_ref[s, :, start : start + wide] = mixed[
                s * per_step : (s + 1) * per_step
            ].astype(jnp.bfloat16)
        after = mixed[token_rows:]
        ends[low] = (ends[low][0] + after, wide) if low in ends else (after, wide)
        everything += last[p]
    for low, (mixed, wide) in ends.items():
        for s in range(steps):
            out_ref[s, :, low : low + wide] = mixed[s * per_step : (s + 1) * per_step].astype(
                jnp.bfloat16
            )
    while stage_of[0] < len(orders[0]):
        advance()
    for copy in everything:
        copy.wait_send()


def layer(slot_table, move_key, kv, moe_in, expert_ids, expert_weights, w_gate, w_up, w_down):
    steps, token_count, width = moe_in.shape
    devices = lax.axis_size("ep")
    groups = devices // SPLIT
    rows = steps * token_count
    columns = part_columns(width, token_count)
    hidden = w_gate.shape[1]
    slot_rows = groups * rows
    moves = move_key.shape[0]
    high = list(range(4, devices.bit_length() - 1))
    orders = ([1] + high + [3, 2, 0], [2, 3] + high + [1, 0])
    bf16 = jnp.bfloat16
    payload = (moves,) + kv.shape[1:]
    scratch = [pltpu.VMEM(payload, bf16), pltpu.VMEM((len(orders[0]),) + payload, bf16)]
    scratch += [pltpu.VMEM((width, 2 * hidden), bf16), pltpu.VMEM((hidden, width), bf16)]
    outer, inner = (groups, rows), (SPLIT, slot_rows)
    for shape in (outer, outer, inner, inner, inner, outer, outer):
        scratch += [pltpu.VMEM(shape + (wide,), bf16) for _, _, wide in columns]
    copies = len(columns) * (2 * (groups - 1) + 13) + len(orders) * len(orders[0])
    scratch += [pltpu.SemaphoreType.DMA((3,))] + [pltpu.SemaphoreType.DMA((copies,))] * 2
    vmem, anywhere = pl.BlockSpec(memory_space=pltpu.VMEM), pl.BlockSpec(memory_space=pl.ANY)
    smem = pl.BlockSpec(memory_space=pltpu.SMEM)
    out, arrivals = pl.pallas_call(
        functools.partial(layer_kernel, groups, columns, orders),
        out_shape=[
            jax.ShapeDtypeStruct(moe_in.shape, bf16),
            jax.ShapeDtypeStruct(payload, bf16),
        ],
        in_specs=[smem] * 4 + [vmem, vmem, anywhere, anywhere, anywhere],
        out_specs=[vmem, vmem],
        scratch_shapes=scratch,
        compiler_params=pltpu.CompilerParams(
            collective_id=0, has_side_effects=True, vmem_limit_bytes=60 * 2**20
        ),
        name="layer",
    )(
        slot_table,
        move_key,
        jnp.transpose(expert_ids, (0, 2, 1)),
        jnp.transpose(expert_weights, (0, 2, 1)),
        kv,
        moe_in,
        w_gate,
        w_up,
        w_down,
    )
    return out, arrivals


def attend_kernel(
    me_ref, slot_ref, key_ref, len_ref, kv_ref, arr_ref, q_ref, new_ref, out_ref, cache_ref
):
    me, moves = me_ref[0], arr_ref.shape[0]
    together = kv_ref.shape[0]
    slots = pl.num_programs(0) * together
    steps, heads = q_ref.shape[0], q_ref.shape[3]
    positions = kv_ref.shape[2]
    owner = lax.broadcasted_iota(jnp.int32, (new_ref.shape[1], positions), 0)
    place = lax.broadcasted_iota(jnp.int32, (new_ref.shape[1], positions), 1)
    at = lax.broadcasted_iota(jnp.int32, (steps * heads, positions), 1)
    step = lax.broadcasted_iota(jnp.int32, (steps * heads, positions), 0) // heads
    column = lax.broadcasted_iota(jnp.int32, (1, positions), 1)
    for n in range(together):
        r = pl.program_id(0) * together + n
        length = len_ref[me * slots + r]
        rows = kv_ref[n]
        for k in range(moves):
            here = slot_ref[k, me] == r
            partner = me ^ key_ref[k]
            length = jnp.where(here, len_ref[partner * slots + slot_ref[k, partner]], length)
            rows = jnp.where(here, arr_ref[k], rows)
        fresh = None
        for s in range(steps):
            spread = jnp.where((owner == r) & (place == length + s), 1.0, 0.0).astype(jnp.bfloat16)
            piece = lax.dot_general(
                new_ref[s], spread, (((0,), (0,)), ((), ())), preferred_element_type=jnp.float32
            )
            fresh = piece if fresh is None else fresh + piece
        keep = jnp.where((column >= length) & (column < length + steps), 0.0, 1.0)
        rows = rows * keep.astype(jnp.bfloat16) + fresh.astype(jnp.bfloat16)
        cache_ref[n] = rows
        merged = jnp.concatenate([q_ref[s, n] for s in range(steps)], axis=1)
        scores = (
            lax.dot_general(
                merged, rows, (((0,), (0,)), ((), ())), preferred_element_type=jnp.float32
            )
            * softmax_scale
        )
        scores = jnp.where(at < length + step + 1, scores, jnp.float32(-1e30))
        weights = jnp.exp(scores - jnp.max(scores, axis=-1, keepdims=True))
        inverse = 1.0 / jnp.sum(weights, axis=-1, keepdims=True)
        attended = lax.dot_general(
            (weights * inverse).astype(jnp.bfloat16),
            rows[:LAT],
            (((1,), (1,)), ((), ())),
            preferred_element_type=jnp.float32,
        ).astype(jnp.bfloat16)
        for s in range(steps):
            out_ref[s, n] = attended[s * heads : (s + 1) * heads]


def attend(me, slot_table, move_key, cache_len, kv, arrivals, queries, new_latent):
    slots, width, positions = kv.shape
    steps, _, _, heads = queries.shape
    moves = arrivals.shape[0]
    together = 2
    grid = pltpu.PrefetchScalarGridSpec(
        num_scalar_prefetch=4,
        grid=(slots // together,),
        in_specs=[
            pl.BlockSpec((together, width, positions), lambda r, *_: (r, 0, 0)),
            pl.BlockSpec((moves, width, positions), lambda r, *_: (0, 0, 0)),
            pl.BlockSpec((steps, together, width, heads), lambda r, *_: (0, r, 0, 0)),
            pl.BlockSpec(new_latent.shape, lambda r, *_: (0, 0, 0)),
        ],
        out_specs=[
            pl.BlockSpec((steps, together, heads, LAT), lambda r, *_: (0, r, 0, 0)),
            pl.BlockSpec((together, width, positions), lambda r, *_: (r, 0, 0)),
        ],
    )
    return pl.pallas_call(
        attend_kernel,
        grid_spec=grid,
        out_shape=[
            jax.ShapeDtypeStruct((steps, slots, heads, LAT), jnp.bfloat16),
            jax.ShapeDtypeStruct(kv.shape, jnp.bfloat16),
        ],
        compiler_params=pltpu.CompilerParams(vmem_limit_bytes=60 * 2**20),
        name="attend",
    )(
        me,
        slot_table,
        move_key,
        cache_len,
        kv,
        arrivals,
        queries,
        new_latent,
    )


def body(
    kv_cache,
    cache_len,
    move_slot,
    move_key,
    queries,
    new_latent,
    moe_in,
    expert_ids,
    expert_weights,
    w_gate,
    w_up,
    w_down,
):
    me = lax.axis_index("ep").reshape(1)
    slot_table = jnp.transpose(move_slot)
    kv = jnp.transpose(kv_cache, (0, 2, 1))
    moe_out, arrivals = layer(
        slot_table, move_key, kv, moe_in, expert_ids, expert_weights, w_gate, w_up, w_down
    )
    attention_out, cache = attend(
        me,
        slot_table,
        move_key,
        cache_len,
        kv,
        arrivals,
        jnp.transpose(queries, (0, 1, 3, 2)),
        new_latent,
    )
    return (attention_out, jnp.transpose(cache, (0, 2, 1)), moe_out)


def solution(mesh):
    in_specs = (
        P(("rep", "ep"), None, None),
        P("rep"),
        P("rep", None),
        P("rep"),
        P(None, ("rep", "ep"), None, None),
        P(None, ("rep", "ep"), None),
        P(None, ("rep", "ep"), None),
        P(None, ("rep", "ep"), None),
        P(None, ("rep", "ep"), None),
        P(None, "ep"),
        P(None, "ep"),
        P("ep", None),
    )
    out_specs = (
        P(None, ("rep", "ep"), None, None),
        P(("rep", "ep"), None, None),
        P(None, ("rep", "ep"), None),
    )
    return jax.shard_map(body, mesh=mesh, in_specs=in_specs, out_specs=out_specs, check_vma=False)
```
